32 devices in a mesh: dp: 4 (over x, core), row: 2 (over y), col: 4 (over z).
Axes of the slice: x: 2, y: 2, z: 4, core: 2. Of those that a mesh axis runs over, the one named last changes fastest.
Arguments:
- activations: bfloat16 [8192, 8192], P('dp', 'row'), may hold values from -24 to 24
- out_grads: bfloat16 [8192, 16384], P(('dp', 'row'), 'col'), may hold values from -24 to 24
- weights: float32 [16384, 8192], P(('col', 'dp'), 'row'), may hold values from -0.0625 to 0.0625
- momentum: bfloat16 [16384, 8192], P(('col', 'dp'), 'row'), may hold values from -3 to 3
- scores: float32 [16384, 8192], P(('col', 'dp'), 'row'), may hold values from -6 to 6
- row_moment: float32 [16384], P(('col', 'dp')), may hold values from 0.05 to 90
- col_moment: float32 [8192], P('row'), may hold values from 0.05 to 90
Outputs:
- weights_new: float32 [16384, 8192], P(('col', 'dp'), 'row')
- momentum_new: bfloat16 [16384, 8192], P(('col', 'dp'), 'row')
- scores_new: float32 [16384, 8192], P(('col', 'dp'), 'row')
- row_moment_new: float32 [16384], P(('col', 'dp'))
- col_moment_new: float32 [8192], P('row')
The draws below stay inside these ranges and needn't reach their ends.
All inputs are finite; a program needn't handle non-finite values.
Results may differ from the reference program's by a relative error of at most 0.004.
Values may be sent and summed in bfloat16 or wider, within the bound.
A program may use at most 256 MiB of HBM per device.

```python
import math
import jax
import jax.numpy as jnp
from jax import lax

D = 8192
FF = 16384
TOKENS = 8192


def column_scale(key, length):
    rising = jnp.exp(math.log(3.0) * jnp.arange(length, dtype=jnp.float32) / length)
    spread = jnp.exp(jax.random.uniform(jax.random.fold_in(key, 21), (length,), jnp.float32, math.log(0.5), math.log(2.0)))
    return rising * spread


def moment_law(key, length):
    place = jnp.arange(length, dtype=jnp.int32)
    rising = jnp.exp(math.log(3.0) * place.astype(jnp.float32) / length)
    ladder = jnp.exp(math.log(0.1) + math.log(300.0) * jnp.arange(16, dtype=jnp.float32) / 15.0)
    order = jax.random.permutation(jax.random.fold_in(key, 31), 16)
    levels = ladder[order]
    block = place * 16 // length
    spread = jnp.exp(jax.random.uniform(jax.random.fold_in(key, 32), (length,), jnp.float32, math.log(0.5), 0.0))
    return levels[block] * rising * spread


def draw_activations(key, part):
    key = jax.random.fold_in(key, 1)
    scaling = column_scale(key, D)
    value_key = jax.random.fold_in(key, 5)
    values = jnp.clip(jax.random.normal(value_key, (TOKENS, D), jnp.float32), -4.0, 4.0)
    return (values * scaling[None, :]).astype(jnp.bfloat16)


def draw_out_grads(key, part):
    key = jax.random.fold_in(key, 2)
    scaling = column_scale(key, FF)
    value_key = jax.random.fold_in(key, 5)
    values = jnp.clip(jax.random.normal(value_key, (TOKENS, FF), jnp.float32), -4.0, 4.0)
    return (values * scaling[None, :]).astype(jnp.bfloat16)


def draw_row_moment(key, part):
    key = jax.random.fold_in(key, 3)
    return moment_law(key, FF)


def draw_col_moment(key, part):
    key = jax.random.fold_in(key, 4)
    return moment_law(key, D)


def level_of(rng, extent, split, least, high):
    def one(dim, shards_of):
        heights = jax.random.uniform(jax.random.fold_in(jax.random.fold_in(rng, 6), dim), (shards_of,), jnp.float32, least / len(split), high / len(split))
        return jnp.repeat(jnp.exp(heights), extent[dim] // shards_of).reshape((-1,) + (1,) * (len(extent) - dim - 1))

    factor_of = one(*split[0])
    for cut in split[1:]:
        factor_of = factor_of * one(*cut)
    return factor_of


def noise(own_key, shape, deviation, bound, cuts=(), kind=jnp.bfloat16):
    array = deviation * jax.random.normal(own_key, shape, jnp.float32)
    if cuts:
        array = array * level_of(own_key, shape, cuts, -0.22, 0.18)
    return jnp.clip(array, -bound, bound).astype(kind)


def setup_inputs(seed: int = 0) -> dict:
    key_of = jax.random.split(jax.random.key(seed), 8)
    activations = draw_activations(jax.random.fold_in(key_of[7], 71), 0)
    out_grads = draw_out_grads(jax.random.fold_in(key_of[7], 71), 0)
    weights = noise(key_of[2], (FF, D), D ** -0.5, 0.0625, ((0, 16), (1, 2)), jnp.float32)
    momentum = noise(key_of[3], (FF, D), 0.5, 3.0, ((0, 16), (1, 2)))
    scores = noise(key_of[4], (FF, D), 1.0, 6.0, ((0, 16), (1, 2)), jnp.float32)
    row_moment = draw_row_moment(jax.random.fold_in(key_of[7], 71), 0)
    col_moment = draw_col_moment(jax.random.fold_in(key_of[7], 71), 0)
    return dict(activations=activations, out_grads=out_grads, weights=weights, momentum=momentum, scores=scores, row_moment=row_moment, col_moment=col_moment)


def reference(activations, out_grads, weights, momentum, scores, row_moment, col_moment):
    act_wide = activations.astype(jnp.float32)
    grad_wide = out_grads.astype(jnp.float32)
    gradient = jnp.dot(grad_wide.T, act_wide, precision=lax.Precision.HIGHEST) * (1.0 / math.sqrt(TOKENS))
    squares = gradient * gradient + 1e-30
    row_moment_new = 0.8 * row_moment + 0.2 * lax.optimization_barrier(jnp.sum(squares, axis=1)) / D
    col_moment_new = 0.8 * col_moment + 0.2 * lax.optimization_barrier(jnp.sum(squares, axis=0)) / FF
    row_mean = jnp.sum(row_moment_new) / FF
    update = gradient * lax.rsqrt(row_moment_new[:, None] * col_moment_new[None, :] / row_mean)
    momentum_new = (0.9 * momentum.astype(jnp.float32) + 0.1 * update).astype(jnp.bfloat16)
    weights_new = weights - 0.01 * momentum_new.astype(jnp.float32)
    scores_new = scores - 50.0 * weights * gradient
    return (weights_new, momentum_new, scores_new, row_moment_new, col_moment_new)
```

```python
import math

import jax
import jax.numpy as jnp
from jax import lax
from jax.sharding import PartitionSpec as P

D = 8192
FF = 16384

PIECES = 4


def token_product(grad_rows, act_rows):
    return lax.dot_general(
        grad_rows, act_rows, (((0,), (0,)), ((), ())), preferred_element_type=jnp.float32
    )


def local(activations, out_grads, weights, momentum, scores, row_moment, col_moment):
    replicas = lax.axis_size("dp")
    token_scale = 1.0 / math.sqrt(activations.shape[0] * replicas)
    me = lax.axis_index("dp")
    core = me % 2
    same_chip = [(i, i ^ 1) for i in range(replicas)]
    other_chip = [(i, i ^ 2) for i in range(replicas)]
    block = out_grads.shape[1] // replicas
    piece = block // PIECES

    act_pair = lax.ppermute(activations, "dp", same_chip)

    def columns(owner, j):
        return lax.dynamic_slice_in_dim(out_grads, owner * block + j * piece, piece, 1)

    def gathered(chip, j):
        mine = columns(2 * chip + core, j)
        theirs = lax.ppermute(columns(2 * chip + 1 - core, j), "dp", same_chip)
        both = jnp.concatenate([mine, theirs], axis=1)
        return lax.all_gather(both, "row", axis=0, tiled=True)

    def chip_sum(chip, j):
        both = gathered(chip, j)
        return token_product(both[:, :piece], activations) + token_product(both[:, piece:], act_pair)

    chip = me // 2
    received = []
    for j in range(PIECES):
        partial = chip_sum(1 - chip, j).astype(jnp.bfloat16)
        received.append(lax.ppermute(partial, "dp", other_chip))
    gradients = []
    row_parts = []
    col_part = 0.0
    for j in range(PIECES):
        own = chip_sum(chip, j)
        g = (own + received[j].astype(jnp.float32)) * token_scale
        squares = g * g + 1e-30
        gradients.append(g)
        row_parts.append(jnp.sum(squares, axis=1))
        col_part = col_part + jnp.sum(squares, axis=0)
    row_full = lax.psum(jnp.concatenate(row_parts), "row")
    row_moment_new = 0.8 * row_moment + 0.2 * row_full / D
    col_full = lax.psum(col_part, ("dp", "col"))
    row_sum = lax.psum(jnp.sum(row_moment_new), ("dp", "col"))
    col_moment_new = 0.8 * col_moment + 0.2 * col_full / FF
    row_average = row_sum / FF
    gradient = jnp.concatenate(gradients, axis=0)
    update = gradient * lax.rsqrt(row_moment_new[:, None] * col_moment_new[None, :] / row_average)
    momentum_new = (0.9 * momentum.astype(jnp.float32) + 0.1 * update).astype(jnp.bfloat16)
    weights_new = weights - 0.01 * momentum_new.astype(jnp.float32)
    scores_new = scores - 50.0 * weights * gradient
    return (weights_new, momentum_new, scores_new, row_moment_new, col_moment_new)


def solution(mesh):
    return jax.shard_map(
        local,
        mesh=mesh,
        in_specs=(
            P("dp", "row"),
            P(("dp", "row"), "col"),
            P(("col", "dp"), "row"),
            P(("col", "dp"), "row"),
            P(("col", "dp"), "row"),
            P(("col", "dp")),
            P("row"),
        ),
        out_specs=(
            P(("col", "dp"), "row"),
            P(("col", "dp"), "row"),
            P(("col", "dp"), "row"),
            P(("col", "dp")),
            P("row"),
        ),
        check_vma=False,
    )
```

```python
import math

import jax
import jax.numpy as jnp
from jax import lax
from jax.sharding import PartitionSpec as P

D = 8192
FF = 16384

ORDER = (("send", 1), ("send", 1), ("send", 2), ("own", 2), ("send", 2), ("own", 2), ("send", 2), ("own", 2), ("own", 2))
AFTER = {2: 0, 3: 1, 5: 2, 7: 3}
IN_FLIGHT = 3


def token_product(grad_rows, act_rows):
    return lax.dot_general(
        grad_rows, act_rows, (((0,), (0,)), ((), ())), preferred_element_type=jnp.float32
    )


def swap(x, axis, bit):
    return lax.ppermute(x, axis, [(i, i ^ bit) for i in range(lax.axis_size(axis))])


def pair_sum(x, axis):
    bit = 1
    while bit < lax.axis_size(axis):
        x = x + swap(x, axis, bit)
        bit *= 2
    return x


def local(activations, out_grads, weights, momentum, scores, row_moment, col_moment):
    replicas = lax.axis_size("dp")
    rows = lax.axis_size("row")
    token_scale = 1.0 / math.sqrt(activations.shape[0] * replicas)
    me = lax.axis_index("dp")
    core, chip = me % 2, me // 2
    block = out_grads.shape[1] // replicas
    unit = block // 8

    pieces = []
    done = {"send": 0, "own": 0}
    for kind, size in ORDER:
        pieces.append((1 - chip if kind == "send" else chip, done[kind] * unit, size * unit))
        done[kind] += size

    def columns(target, of, start, size):
        return lax.dynamic_slice_in_dim(out_grads, (2 * target + of) * block + start, size, 1)

    held = []
    for target, start, size in pieces:
        theirs = swap(columns(target, 1 - core, start, size), "dp", 1)
        held.append((columns(target, core, start, size), theirs))
    first, act_mine = lax.optimization_barrier((held[0], activations))
    held[0] = first
    act_pair = swap(act_mine, "dp", 1)

    def over_row(pair):
        if rows == 2:
            return tuple(swap(h, "row", 1) for h in pair)
        return tuple(lax.all_gather(h, "row", axis=0, tiled=True) for h in pair)

    upper = lax.axis_index("row") == 1

    def tokens(mine, came):
        if rows != 2:
            return came
        return jnp.concatenate([jnp.where(upper, came, mine), jnp.where(upper, mine, came)], axis=0)

    arriving = [over_row(pair) for pair in held[:IN_FLIGHT]]
    received, own = [], []
    for k, (kind, _) in enumerate(ORDER):
        if k in AFTER:
            sent = AFTER[k]
            arriving[k], received[sent] = lax.optimization_barrier((arriving[k], received[sent]))
        lhs, lhs_pair = (tokens(m, c) for m, c in zip(held[k], arriving[k]))
        total = token_product(lhs, activations) + token_product(lhs_pair, act_pair)
        if kind == "send":
            total = total.astype(jnp.bfloat16)
        if k + 1 < len(pieces):
            total, arriving[k + 1] = lax.optimization_barrier((total, arriving[k + 1]))
        if k + IN_FLIGHT < len(pieces):
            total, following = lax.optimization_barrier((total, held[k + IN_FLIGHT]))
            arriving.append(over_row(following))
        if kind == "send":
            received.append(swap(total, "dp", 2))
        else:
            own.append(total)

    received = [jnp.concatenate(received[:2], axis=0)] + received[2:]
    gradients, row_parts = [], []
    col_part = 0.0
    for mine, came in zip(own, received):
        g = (mine + came.astype(jnp.float32)) * token_scale
        squares = g * g + 1e-30
        gradients.append(g)
        row_parts.append(jnp.sum(squares, axis=1))
        col_part = col_part + jnp.sum(squares, axis=0)
    row_part = jnp.concatenate(row_parts)
    row_full = pair_sum(row_part, "row") if rows == 2 else lax.psum(row_part, "row")
    row_moment_new = 0.8 * row_moment + 0.2 * row_full / D
    tail = jnp.full((128,), jnp.sum(row_moment_new), jnp.float32)
    sums = pair_sum(pair_sum(jnp.concatenate([col_part, tail]), "dp"), "col")
    col_full, row_sum = sums[:-128], sums[-1]
    col_moment_new = 0.8 * col_moment + 0.2 * col_full / FF
    row_average = row_sum / FF
    gradient = jnp.concatenate(gradients, axis=0)
    update = gradient * lax.rsqrt(row_moment_new[:, None] * col_moment_new[None, :] / row_average)
    momentum_new = (0.9 * momentum.astype(jnp.float32) + 0.1 * update).astype(jnp.bfloat16)
    weights_new = weights - 0.01 * momentum_new.astype(jnp.float32)
    scores_new = scores - 50.0 * weights * gradient
    return (weights_new, momentum_new, scores_new, row_moment_new, col_moment_new)


def solution(mesh):
    return jax.shard_map(
        local,
        mesh=mesh,
        in_specs=(
            P("dp", "row"),
            P(("dp", "row"), "col"),
            P(("col", "dp"), "row"),
            P(("col", "dp"), "row"),
            P(("col", "dp"), "row"),
            P(("col", "dp")),
            P("row"),
        ),
        out_specs=(
            P(("col", "dp"), "row"),
            P(("col", "dp"), "row"),
            P(("col", "dp"), "row"),
            P(("col", "dp")),
            P("row"),
        ),
        check_vma=False,
    )
```

```python
import math

import jax
import jax.numpy as jnp
from jax import lax
from jax.sharding import PartitionSpec as P

D = 8192
FF = 16384

ORDER = (("send", 1), ("send", 1), ("send", 2), ("own", 2), ("send", 2), ("send", 2), ("own", 2), ("own", 2), ("own", 2))
AFTER = {2: 0, 3: 1, 4: 2, 5: 3, 6: 4, 7: 5, 8: 6}
IN_FLIGHT = 3


def token_product(grad_rows, act_rows):
    return lax.dot_general(
        grad_rows, act_rows, (((0,), (0,)), ((), ())), preferred_element_type=jnp.float32
    )


def swap(x, axis, bit):
    return lax.ppermute(x, axis, [(i, i ^ bit) for i in range(lax.axis_size(axis))])


def pair_sum(x, axis):
    bit = 1
    while bit < lax.axis_size(axis):
        x = x + swap(x, axis, bit)
        bit *= 2
    return x


def local(activations, out_grads, weights, momentum, scores, row_moment, col_moment):
    replicas = lax.axis_size("dp")
    rows = lax.axis_size("row")
    token_scale = 1.0 / math.sqrt(activations.shape[0] * replicas)
    me = lax.axis_index("dp")
    core, chip = me % 2, me // 2
    block = out_grads.shape[1] // replicas
    unit = block // 8

    pieces = []
    done = {"send": 0, "own": 0}
    for kind, size in ORDER:
        pieces.append((1 - chip if kind == "send" else chip, done[kind] * unit, size * unit))
        done[kind] += size

    def columns(target, of, start, size):
        return lax.dynamic_slice_in_dim(out_grads, (2 * target + of) * block + start, size, 1)

    held = []
    for target, start, size in pieces:
        theirs = swap(columns(target, 1 - core, start, size), "dp", 1)
        held.append((columns(target, core, start, size), theirs))
    first, act_mine = lax.optimization_barrier((held[0], activations))
    held[0] = first
    act_pair = swap(act_mine, "dp", 1)

    def over_row(pair):
        if rows == 2:
            return tuple(swap(h, "row", 1) for h in pair)
        return tuple(lax.all_gather(h, "row", axis=0, tiled=True) for h in pair)

    upper = lax.axis_index("row") == 1

    def tokens(mine, came):
        if rows != 2:
            return came
        return jnp.concatenate([jnp.where(upper, came, mine), jnp.where(upper, mine, came)], axis=0)

    arriving = [over_row(pair) for pair in held[:IN_FLIGHT]]
    received, own = [], []
    for k, (kind, _) in enumerate(ORDER):
        if k in AFTER:
            sent = AFTER[k]
            arriving[k], received[sent] = lax.optimization_barrier((arriving[k], received[sent]))
        lhs, lhs_pair = (tokens(m, c) for m, c in zip(held[k], arriving[k]))
        total = token_product(lhs, activations) + token_product(lhs_pair, act_pair)
        if kind == "send":
            total = total.astype(jnp.bfloat16)
        if k + 1 < len(pieces):
            total, arriving[k + 1] = lax.optimization_barrier((total, arriving[k + 1]))
        if k + IN_FLIGHT < len(pieces):
            total, following = lax.optimization_barrier((total, held[k + IN_FLIGHT]))
            arriving.append(over_row(following))
        if kind == "send":
            for row in range(0, total.shape[0], unit):
                received.append(swap(lax.slice_in_dim(total, row, row + unit, axis=0), "dp", 2))
        else:
            own.append(total)

    received = [jnp.concatenate(received[k : k + 2], axis=0) for k in range(0, len(received), 2)]
    gradients, row_parts = [], []
    col_part = 0.0
    scores_new = jnp.zeros_like(scores)
    start = 0
    for mine, came in zip(own, received):
        g = (mine + came.astype(jnp.float32)) * token_scale
        squares = g * g + 1e-30
        gradients.append(g)
        at = slice(start, start + g.shape[0])
        scores_new = scores_new.at[at].set(scores[at] - 50.0 * weights[at] * g)
        start += g.shape[0]
        row_parts.append(jnp.sum(squares, axis=1))
        col_part = col_part + jnp.sum(squares, axis=0)
    row_part = jnp.concatenate(row_parts)
    row_full = pair_sum(row_part, "row") if rows == 2 else lax.psum(row_part, "row")
    row_moment_new = 0.8 * row_moment + 0.2 * row_full / D
    tail = jnp.full((128,), jnp.sum(row_moment_new), jnp.float32)
    sums = pair_sum(pair_sum(jnp.concatenate([col_part, tail]), "dp"), "col")
    col_full, row_sum = sums[:-128], sums[-1]
    col_moment_new = 0.8 * col_moment + 0.2 * col_full / FF
    row_average = row_sum / FF
    gradient = jnp.concatenate(gradients, axis=0)
    update = gradient * lax.rsqrt(row_moment_new[:, None] * col_moment_new[None, :] / row_average)
    momentum_new = (0.9 * momentum.astype(jnp.float32) + 0.1 * update).astype(jnp.bfloat16)
    weights_new = weights - 0.01 * momentum_new.astype(jnp.float32)
    return (weights_new, momentum_new, scores_new, row_moment_new, col_moment_new)


def solution(mesh):
    return jax.shard_map(
        local,
        mesh=mesh,
        in_specs=(
            P("dp", "row"),
            P(("dp", "row"), "col"),
            P(("col", "dp"), "row"),
            P(("col", "dp"), "row"),
            P(("col", "dp"), "row"),
            P(("col", "dp")),
            P("row"),
        ),
        out_specs=(
            P(("col", "dp"), "row"),
            P(("col", "dp"), "row"),
            P(("col", "dp"), "row"),
            P(("col", "dp")),
            P("row"),
        ),
        check_vma=False,
    )
```
